256 devices in a mesh: dp: 4 (over x), cent: 64 (over z, y, core).
Axes of the slice: x: 4, y: 4, z: 8, core: 2. Of those that a mesh axis runs over, the one named last changes fastest.
Arguments:
- embeddings: bfloat16 [8192, 1024], P('dp'), may hold values from -64 to 64
- centroids: bfloat16 [32768, 1024], P('cent'), may hold values from -2 to 2
Outputs:
- new_centroids: float32 [32768, 1024], P('cent', 'dp')
- log_totals: float32 [8192], P('dp')
The draws below stay inside these ranges and needn't reach their ends.
All inputs are finite; a program needn't handle non-finite values.
Results may differ from the reference program's by a relative error of at most 0.012.
Values may be sent and summed in bfloat16 or wider, within the bound.
No kernel may reach another device: no remote copies, remote signals or barrier semaphores. Data moves between devices by JAX's collectives and lax.ppermute only.
A program may use at most 64 MiB of HBM per device.

```python
import math
import jax
import jax.numpy as jnp
from jax import lax

D = 1024
E_DEV = 2048
BLOCK = 512
CENTROIDS = 32768
EMB = 8192
N_DP = 4


def centroid_base(key):
    return 0.15 * jax.random.normal(key, (CENTROIDS, D), jnp.float32)


def draw_centroids(key, part):
    base_draw = centroid_base(key)
    return base_draw.astype(jnp.bfloat16)


def draw_embeddings(key, part):
    key = jax.random.fold_in(key, 23)
    key_rough = jax.random.fold_in(key, 0)
    return jax.random.normal(key_rough, (EMB, D), jnp.float32).astype(jnp.bfloat16)


def setup_inputs(seed: int = 0) -> dict:
    keys = jax.random.split(jax.random.key(seed), 3)
    embeddings = draw_embeddings(jax.random.fold_in(keys[2], 71), 0)
    centroids = draw_centroids(jax.random.fold_in(keys[2], 71), 0)
    return {"embeddings": embeddings, "centroids": centroids}


softness_level = 0.1
prior_mass = 4.0

def block_logits(embedding_row_tile, centroids, squared_norms):
    inner_products = lax.dot_general(embedding_row_tile, centroids, (((1,), (1,)), ((), ())), preferred_element_type=jnp.float32)
    return (2.0 * inner_products - squared_norms[None, :]) / (softness_level * math.sqrt(embedding_row_tile.shape[1]))

def reference(embeddings, centroids):
    cent_f = centroids.astype(jnp.float32)
    squared_norms = lax.optimization_barrier(jnp.sum(cent_f * cent_f, axis=1))
    numerator = jnp.zeros((CENTROIDS, D), jnp.float32)
    mass_sum = jnp.zeros((CENTROIDS,), jnp.float32)
    lse_pieces = []
    for shard_index in range(N_DP):
        shard_rows = embeddings[shard_index * E_DEV:(shard_index + 1) * E_DEV].reshape(E_DEV // BLOCK, BLOCK, D)

        def scan_step(running, embedding_row_tile):
            part_numer, shard_assignment_mass = running
            logits = block_logits(embedding_row_tile, centroids, squared_norms)
            row_top = lax.optimization_barrier(jnp.max(logits, axis=1))
            log_total = row_top + jnp.log(lax.optimization_barrier(jnp.sum(jnp.exp(logits - row_top[:, None]), axis=1)))
            weights = jnp.exp(logits - log_total[:, None]).astype(jnp.bfloat16)
            part_numer = part_numer + lax.dot_general(weights, embedding_row_tile, (((0,), (0,)), ((), ())), preferred_element_type=jnp.float32)
            shard_assignment_mass = shard_assignment_mass + lax.optimization_barrier(jnp.sum(weights.astype(jnp.float32), axis=0))
            return ((part_numer, shard_assignment_mass), log_total)
        start_state = (jnp.zeros((CENTROIDS, D), jnp.float32), jnp.zeros((CENTROIDS,), jnp.float32))
        (part_numer, shard_assignment_mass), log_total = lax.scan(scan_step, start_state, shard_rows)
        numerator = numerator + lax.optimization_barrier(part_numer.astype(jnp.bfloat16)).astype(jnp.float32)
        mass_sum = mass_sum + lax.optimization_barrier(shard_assignment_mass.astype(jnp.bfloat16)).astype(jnp.float32)
        lse_pieces.append(log_total.reshape(E_DEV))
    new_centroids = (numerator + prior_mass * cent_f) / (mass_sum[:, None] + prior_mass)
    return (new_centroids, jnp.concatenate(lse_pieces))
```

```python
import functools
import math

import jax
import jax.numpy as jnp
from jax import lax
from jax.experimental import pallas as pl
from jax.experimental.pallas import tpu as pltpu
from jax.sharding import Mesh, PartitionSpec as P

SOFTNESS = 0.1
PRIOR = 4.0
LOG2E = math.log2(math.e)
LN2 = math.log(2.0)
ROWS = 256
VMEM_LIMIT = 56 * 1024 * 1024


def logits_kernel(scale, emb_ref, cent_ref, z_ref, lse_ref, half_sq):
    step = pl.program_id(0)

    @pl.when(step == 0)
    def _():
        c = cent_ref[...].astype(jnp.float32)
        half_sq[...] = 0.5 * jnp.sum(c * c, axis=1, keepdims=True)

    inner = lax.dot_general(
        cent_ref[...], emb_ref[...], (((1,), (1,)), ((), ())), preferred_element_type=jnp.float32
    )
    z = (inner - half_sq[...]) * scale
    z_ref[...] = z
    top = jnp.max(z, axis=0, keepdims=True)
    total = jnp.sum(jnp.exp2(z - top), axis=0, keepdims=True)
    lse = top + jnp.log2(total)
    lse_ref[...] = jnp.broadcast_to(lse, lse_ref.shape)


def weights_kernel(n_dp, z_ref, tot_ref, emb_ref, out_ref, w_ref):
    cents, rows = z_ref.shape
    cols = emb_ref.shape[1] // n_dp
    mass = jnp.zeros((cents, 128), jnp.float32)
    for r in range(rows // 128):
        w = jnp.exp2(z_ref[:, r * 128 : (r + 1) * 128] - tot_ref[r : r + 1, :]).astype(jnp.bfloat16)
        w_ref[:, r * 128 : (r + 1) * 128] = w
        mass = mass + w.astype(jnp.float32)
    mass = jnp.broadcast_to(jnp.sum(mass, axis=1, keepdims=True), (cents, 128)).T
    mass_rows = jnp.concatenate([mass[:8, :cols], mass[:8, cols:]], axis=0).astype(jnp.bfloat16)
    for d in range(n_dp):
        out_ref[d, :cents, :] = jnp.dot(
            w_ref[...], emb_ref[:, d * cols : (d + 1) * cols], preferred_element_type=jnp.float32
        ).astype(jnp.bfloat16)
        out_ref[d, cents:, :] = mass_rows


def update_kernel(parts_ref, prior_ref, out_ref):
    n_dp = parts_ref.shape[0]
    cents, cols = out_ref.shape
    total = PRIOR * prior_ref[...].astype(jnp.float32)
    mass = jnp.full((16, cols), PRIOR, jnp.float32)
    for d in range(n_dp):
        total = total + parts_ref[d, :cents, :].astype(jnp.float32)
        mass = mass + parts_ref[d, cents:, :].astype(jnp.float32)
    inv = jnp.concatenate([mass[:1, :], mass[8:9, :]], axis=1)
    inv = 1.0 / jnp.broadcast_to(inv, (128, cents)).T
    for k in range(cols // 128):
        out_ref[:, k * 128 : (k + 1) * 128] = total[:, k * 128 : (k + 1) * 128] * inv


def merge(lse):
    top = jnp.max(lse, axis=0)
    return top + jnp.log2(jnp.sum(jnp.exp2(lse - top), axis=0))


def shards(n_dp, emb, cent):
    rows, width = emb.shape
    cents = cent.shape[0]
    cols = width // n_dp
    scale = 2.0 * LOG2E / (SOFTNESS * math.sqrt(width))
    params = pltpu.CompilerParams(vmem_limit_bytes=VMEM_LIMIT)
    z, lse = pl.pallas_call(
        functools.partial(logits_kernel, scale),
        grid=(rows // ROWS,),
        in_specs=[
            pl.BlockSpec((ROWS, width), lambda i: (i, 0)),
            pl.BlockSpec((cents, width), lambda i: (0, 0)),
        ],
        out_specs=[
            pl.BlockSpec((cents, ROWS), lambda i: (0, i)),
            pl.BlockSpec((8, ROWS), lambda i: (0, i)),
        ],
        out_shape=[
            jax.ShapeDtypeStruct((cents, rows), jnp.float32),
            jax.ShapeDtypeStruct((8, rows), jnp.float32),
        ],
        scratch_shapes=[pltpu.VMEM((cents, 1), jnp.float32)],
        compiler_params=params,
    )(emb, cent)

    core = lax.axis_index("core")
    swap = [(0, 1), (1, 0)]
    half = rows // 2
    lse = lse[0].reshape(2, half // 128, 128)
    keep = lax.dynamic_index_in_dim(lse, core, 0, keepdims=False)
    give = lax.dynamic_index_in_dim(lse, 1 - core, 0, keepdims=False)
    got = lax.ppermute(give, "core", swap)
    pair = merge(jnp.stack([keep, got]))
    peers = lax.axis_size("z") * lax.axis_size("y")
    every = lax.all_to_all(jnp.broadcast_to(pair, (peers,) + pair.shape), ("z", "y"), 0, 0)
    own_half = merge(every)
    other_half = lax.ppermute(own_half, "core", swap)
    totals = jnp.where(
        core == 0,
        jnp.concatenate([own_half, other_half]),
        jnp.concatenate([other_half, own_half]),
    )

    parts = pl.pallas_call(
        functools.partial(weights_kernel, n_dp),
        out_shape=jax.ShapeDtypeStruct((n_dp, cents + 16, cols), jnp.bfloat16),
        scratch_shapes=[pltpu.VMEM((cents, rows), jnp.bfloat16)],
        compiler_params=params,
    )(z, totals, emb)
    parts = lax.all_to_all(parts, "x", 0, 0)
    prior = lax.dynamic_slice_in_dim(cent, lax.axis_index("x") * cols, cols, 1)
    new_centroids = pl.pallas_call(
        update_kernel,
        out_shape=jax.ShapeDtypeStruct((cents, cols), jnp.float32),
        compiler_params=params,
    )(parts, prior)
    return new_centroids, (totals * LN2).reshape(rows)


def solution(mesh):
    n_dp = mesh.shape["dp"]
    fine = Mesh(mesh.devices.reshape(n_dp, 8, 4, 2), ("x", "z", "y", "core"))
    cent = ("z", "y", "core")
    return jax.shard_map(
        functools.partial(shards, n_dp),
        mesh=fine,
        in_specs=(P("x", None), P(cent, None)),
        out_specs=(P(cent, "x"), P("x")),
        check_vma=False,
    )
```

```python
import functools
import math

import jax
import jax.numpy as jnp
from jax import lax
from jax.experimental import pallas as pl
from jax.experimental.pallas import tpu as pltpu
from jax.sharding import Mesh, PartitionSpec as P

SOFTNESS = 0.1
PRIOR = 4.0
LOG2E = math.log2(math.e)
LN2 = math.log(2.0)
ROWS = 256
LOADS = 2
LANES = 128
MASS_ROWS = 16
VMEM_LIMIT = 16 * 1024 * 1024
IN_VMEM = pl.BlockSpec(memory_space=pltpu.VMEM)
IN_HBM = pl.BlockSpec(memory_space=pltpu.HBM)


def in_vmem(x):
    return pltpu.with_memory_space_constraint(x, pltpu.VMEM)


def in_hbm(x):
    return pltpu.with_memory_space_constraint(x, pltpu.HBM)


def logits_kernel(scale, emb_hbm, cent_hbm, z_ref, lse_ref, emb_ref, prior_ref, cent_ref, half_sq, sems):
    rows = emb_ref.shape[0]
    cols = prior_ref.shape[1]
    cent_copy = pltpu.make_async_copy(cent_hbm, cent_ref, sems.at[LOADS])
    cent_copy.start()
    load = rows // LOADS
    copies = []
    for k in range(LOADS):
        part = pl.ds(k * load, load)
        copies.append(pltpu.make_async_copy(emb_hbm.at[part, :], emb_ref.at[part, :], sems.at[k]))
        copies[-1].start()
    cent_copy.wait()
    c = cent_ref[...].astype(jnp.float32)
    half_sq[...] = jnp.broadcast_to(0.5 * jnp.sum(c * c, axis=1, keepdims=True), half_sq.shape)
    first_col = pl.multiple_of(lax.axis_index("x") * cols, cols)
    prior_ref[...] = cent_ref[:, pl.ds(first_col, cols)]
    for r in range(0, rows, ROWS):
        if r % load == 0:
            copies[r // load].wait()
        inner = lax.dot_general(
            cent_ref[...], emb_ref[r : r + ROWS, :], (((1,), (1,)), ((), ())), preferred_element_type=jnp.float32
        )
        z = (inner - half_sq[:, :1]) * scale
        z_ref[:, r : r + ROWS] = z
        top = jnp.max(z, axis=0, keepdims=True)
        lse = top + jnp.log2(jnp.sum(jnp.exp2(z - top), axis=0, keepdims=True))
        for k in range(ROWS // LANES):
            lse_ref[pl.ds(r // LANES + k, 1), :] = lse[:, k * LANES : (k + 1) * LANES]


def merge(lse):
    top = jnp.max(lse, axis=0)
    return top + jnp.log2(jnp.sum(jnp.exp2(lse - top), axis=0))


def weights_kernel(z_ref, every_ref, emb_ref, parts_ref, log_totals_ref, w_ref):
    cents, rows = z_ref.shape
    n_dp, _, cols = parts_ref.shape
    totals = merge(every_ref[...])
    log_totals_ref[...] = totals * LN2
    mass = jnp.zeros((cents, LANES), jnp.float32)
    for k in range(rows // LANES):
        w = jnp.exp2(z_ref[:, k * LANES : (k + 1) * LANES] - totals[k : k + 1, :]).astype(jnp.bfloat16)
        w_ref[:, k * LANES : (k + 1) * LANES] = w
        mass = mass + w.astype(jnp.float32)
    for d in range(n_dp):
        parts_ref[d, :cents, :] = jnp.dot(
            w_ref[...], emb_ref[:, d * cols : (d + 1) * cols], preferred_element_type=jnp.float32
        ).astype(jnp.bfloat16)
    mass = jnp.broadcast_to(jnp.sum(mass, axis=1, keepdims=True), (cents, LANES)).T
    half = MASS_ROWS // 2
    mass = jnp.concatenate([mass[:half, :cols], mass[:half, cols:]], axis=0).astype(jnp.bfloat16)
    for d in range(n_dp):
        parts_ref[d, cents:, :] = mass


def update_kernel(parts_ref, prior_ref, out_ref):
    n_dp = parts_ref.shape[0]
    cents, cols = out_ref.shape
    total = PRIOR * prior_ref[...].astype(jnp.float32)
    mass = jnp.full((MASS_ROWS, cols), PRIOR, jnp.float32)
    for d in range(n_dp):
        total = total + parts_ref[d, :cents, :].astype(jnp.float32)
        mass = mass + parts_ref[d, cents:, :].astype(jnp.float32)
    half = MASS_ROWS // 2
    mass = jnp.concatenate([mass[:1, :], mass[half : half + 1, :]], axis=1)
    inv = 1.0 / jnp.broadcast_to(mass, (LANES, cents)).T
    for k in range(cols // LANES):
        out_ref[:, k * LANES : (k + 1) * LANES] = total[:, k * LANES : (k + 1) * LANES] * inv


def shards(n_dp, emb, cent):
    rows, width = emb.shape
    cents = cent.shape[0]
    cols = width // n_dp
    scale = 2.0 * LOG2E / (SOFTNESS * math.sqrt(width))
    params = pltpu.CompilerParams(vmem_limit_bytes=VMEM_LIMIT)
    z, lse, emb_vmem, prior = pl.pallas_call(
        functools.partial(logits_kernel, scale),
        in_specs=[IN_HBM] * 2,
        out_specs=[IN_VMEM] * 4,
        out_shape=[
            pltpu.VMEM((cents, rows), jnp.float32),
            pltpu.VMEM((rows // LANES, LANES), jnp.float32),
            pltpu.VMEM(emb.shape, emb.dtype),
            pltpu.VMEM((cents, cols), cent.dtype),
        ],
        scratch_shapes=[
            pltpu.VMEM(cent.shape, cent.dtype),
            pltpu.VMEM((cents, LANES), jnp.float32),
            pltpu.SemaphoreType.DMA((LOADS + 1,)),
        ],
        compiler_params=params,
    )(in_hbm(emb), in_hbm(cent))

    other = lax.ppermute(lse, "core", [(0, 1), (1, 0)])
    chip = merge(jnp.stack([lse, other]))
    chips = lax.axis_size("z") * lax.axis_size("y")
    every = lax.all_to_all(jnp.broadcast_to(chip, (chips,) + chip.shape), ("z", "y"), 0, 0)

    parts, log_totals = pl.pallas_call(
        weights_kernel,
        in_specs=[IN_VMEM] * 3,
        out_specs=[IN_VMEM] * 2,
        out_shape=[
            pltpu.VMEM((n_dp, cents + MASS_ROWS, cols), jnp.bfloat16),
            jax.ShapeDtypeStruct(lse.shape, jnp.float32),
        ],
        scratch_shapes=[pltpu.VMEM((cents, rows), jnp.bfloat16)],
        compiler_params=params,
    )(in_vmem(z), in_vmem(every), in_vmem(emb_vmem))
    parts = lax.all_to_all(parts, "x", 0, 0)
    new_centroids = pl.pallas_call(
        update_kernel,
        in_specs=[IN_VMEM] * 2,
        out_specs=IN_VMEM,
        out_shape=jax.ShapeDtypeStruct((cents, cols), jnp.float32),
        compiler_params=params,
    )(in_vmem(parts), in_vmem(prior))
    return new_centroids, log_totals.reshape(rows)


def solution(mesh):
    n_dp = mesh.shape["dp"]
    fine = Mesh(mesh.devices.reshape(n_dp, 8, 4, 2), ("x", "z", "y", "core"))
    cent = ("z", "y", "core")
    return jax.shard_map(
        functools.partial(shards, n_dp),
        mesh=fine,
        in_specs=(P("x", None), P(cent, None)),
        out_specs=(P(cent, "x"), P("x")),
        check_vma=False,
    )
```

```python
import functools
import math

import jax
import jax.numpy as jnp
from jax import lax
from jax.experimental import pallas as pl
from jax.experimental.pallas import tpu as pltpu
from jax.sharding import Mesh, PartitionSpec as P

SOFTNESS = 0.1
PRIOR = 4.0
LOG2E = math.log2(math.e)
LN2 = math.log(2.0)
ROWS = 256
LOADS = 2
LANES = 128
MASS_ROWS = 16
VMEM_LIMIT = 16 * 1024 * 1024
IN_VMEM = pl.BlockSpec(memory_space=pltpu.VMEM)
IN_HBM = pl.BlockSpec(memory_space=pltpu.HBM)


def in_vmem(x):
    return pltpu.with_memory_space_constraint(x, pltpu.VMEM)


def in_hbm(x):
    return pltpu.with_memory_space_constraint(x, pltpu.HBM)


def logits_kernel(scale, emb_hbm, cent_hbm, z_ref, lse_ref, emb_ref, prior_ref, cent_ref, half_sq, sems):
    rows = emb_ref.shape[0]
    cols = prior_ref.shape[1]
    cent_copy = pltpu.make_async_copy(cent_hbm, cent_ref, sems.at[LOADS])
    cent_copy.start()
    load = rows // LOADS
    copies = []
    for k in range(LOADS):
        part = pl.ds(k * load, load)
        copies.append(pltpu.make_async_copy(emb_hbm.at[part, :], emb_ref.at[part, :], sems.at[k]))
        copies[-1].start()
    cent_copy.wait()
    c = cent_ref[...].astype(jnp.float32)
    half_sq[...] = jnp.broadcast_to(0.5 * jnp.sum(c * c, axis=1, keepdims=True), half_sq.shape)
    first_col = pl.multiple_of(lax.axis_index("x") * cols, cols)
    prior_ref[...] = cent_ref[:, pl.ds(first_col, cols)]
    for r in range(0, rows, ROWS):
        if r % load == 0:
            copies[r // load].wait()
        inner = lax.dot_general(
            cent_ref[...], emb_ref[r : r + ROWS, :], (((1,), (1,)), ((), ())), preferred_element_type=jnp.float32
        )
        z = (inner - half_sq[:, :1]) * scale
        z_ref[:, r : r + ROWS] = z
        top = jnp.max(z, axis=0, keepdims=True)
        lse = top + jnp.log2(jnp.sum(jnp.exp2(z - top), axis=0, keepdims=True))
        for k in range(ROWS // LANES):
            lse_ref[pl.ds(r // LANES + k, 1), :] = lse[:, k * LANES : (k + 1) * LANES]


def merge(lse):
    top = jnp.max(lse, axis=0)
    return top + jnp.log2(jnp.sum(jnp.exp2(lse - top), axis=0))


def weights_kernel(shifts, z_ref, every_ref, emb_ref, *refs):
    parts_refs = refs[: len(shifts)]
    w_ref, mass_ref, log_totals_ref = refs[len(shifts) :]
    cents, rows = z_ref.shape
    cols = mass_ref.shape[1]
    n_dp = emb_ref.shape[1] // cols
    totals = merge(every_ref[...])
    log_totals_ref[...] = totals * LN2
    mass = jnp.zeros((cents, LANES), jnp.float32)
    for k in range(rows // LANES):
        w = jnp.exp2(z_ref[:, k * LANES : (k + 1) * LANES] - totals[k : k + 1, :]).astype(jnp.bfloat16)
        w_ref[:, k * LANES : (k + 1) * LANES] = w
        mass = mass + w.astype(jnp.float32)
    me = lax.axis_index("x")
    for shift, parts_ref in zip(shifts, parts_refs):
        first_col = pl.multiple_of(lax.rem(me + shift, n_dp) * cols, cols)
        parts_ref[:cents, :] = jnp.dot(
            w_ref[...], emb_ref[:, pl.ds(first_col, cols)], preferred_element_type=jnp.float32
        ).astype(jnp.bfloat16)
    mass = jnp.broadcast_to(jnp.sum(mass, axis=1, keepdims=True), (cents, LANES)).T
    half = MASS_ROWS // 2
    mass = jnp.concatenate([mass[:half, :cols], mass[:half, cols:]], axis=0).astype(jnp.bfloat16)
    mass_ref[...] = mass
    for parts_ref in parts_refs:
        parts_ref[cents:, :] = mass


def own_kernel(w_ref, emb_ref, prior_ref, out_ref):
    cols = out_ref.shape[1]
    first_col = pl.multiple_of(lax.axis_index("x") * cols, cols)
    own = jnp.dot(w_ref[...], emb_ref[:, pl.ds(first_col, cols)], preferred_element_type=jnp.float32)
    out_ref[...] = own + PRIOR * prior_ref[...].astype(jnp.float32)


def update_kernel(own_ref, mass_ref, *refs):
    parts_refs, out_ref = refs[:-1], refs[-1]
    cents, cols = out_ref.shape
    total = own_ref[...]
    mass = PRIOR + mass_ref[...].astype(jnp.float32)
    for parts_ref in parts_refs:
        total = total + parts_ref[:cents, :].astype(jnp.float32)
        mass = mass + parts_ref[cents:, :].astype(jnp.float32)
    half = MASS_ROWS // 2
    mass = jnp.concatenate([mass[:1, :], mass[half : half + 1, :]], axis=1)
    inv = 1.0 / jnp.broadcast_to(mass, (LANES, cents)).T
    for k in range(cols // LANES):
        out_ref[:, k * LANES : (k + 1) * LANES] = total[:, k * LANES : (k + 1) * LANES] * inv


def shards(n_dp, emb, cent):
    rows, width = emb.shape
    cents = cent.shape[0]
    cols = width // n_dp
    scale = 2.0 * LOG2E / (SOFTNESS * math.sqrt(width))
    params = pltpu.CompilerParams(vmem_limit_bytes=VMEM_LIMIT)
    z, lse, emb_vmem, prior = pl.pallas_call(
        functools.partial(logits_kernel, scale),
        in_specs=[IN_HBM] * 2,
        out_specs=[IN_VMEM] * 4,
        out_shape=[
            pltpu.VMEM((cents, rows), jnp.float32),
            pltpu.VMEM((rows // LANES, LANES), jnp.float32),
            pltpu.VMEM(emb.shape, emb.dtype),
            pltpu.VMEM((cents, cols), cent.dtype),
        ],
        scratch_shapes=[
            pltpu.VMEM(cent.shape, cent.dtype),
            pltpu.VMEM((cents, LANES), jnp.float32),
            pltpu.SemaphoreType.DMA((LOADS + 1,)),
        ],
        compiler_params=params,
    )(in_hbm(emb), in_hbm(cent))

    other = lax.ppermute(lse, "core", [(0, 1), (1, 0)])
    chip = merge(jnp.stack([lse, other]))
    chips = lax.axis_size("z") * lax.axis_size("y")
    every = lax.all_to_all(jnp.broadcast_to(chip, (chips,) + chip.shape), ("z", "y"), 0, 0)

    shifts = [n_dp // 2] + [k for k in range(1, n_dp) if k != n_dp // 2]
    part = pltpu.VMEM((cents + MASS_ROWS, cols), jnp.bfloat16)
    *parts, w, mass, log_totals = pl.pallas_call(
        functools.partial(weights_kernel, shifts),
        in_specs=[IN_VMEM] * 3,
        out_specs=[IN_VMEM] * (len(shifts) + 3),
        out_shape=[part] * len(shifts)
        + [
            pltpu.VMEM((cents, rows), jnp.bfloat16),
            pltpu.VMEM((MASS_ROWS, cols), jnp.bfloat16),
            jax.ShapeDtypeStruct(lse.shape, jnp.float32),
        ],
        compiler_params=params,
    )(in_vmem(z), in_vmem(every), in_vmem(emb_vmem))
    parts = [
        lax.ppermute(p, "x", [(k, (k + shift) % n_dp) for k in range(n_dp)]) for shift, p in zip(shifts, parts)
    ]
    own = pl.pallas_call(
        own_kernel,
        in_specs=[IN_VMEM] * 3,
        out_specs=IN_VMEM,
        out_shape=pltpu.VMEM((cents, cols), jnp.float32),
        compiler_params=params,
    )(in_vmem(w), in_vmem(emb_vmem), in_vmem(prior))
    new_centroids = pl.pallas_call(
        update_kernel,
        in_specs=[IN_VMEM] * (2 + len(parts)),
        out_specs=IN_VMEM,
        out_shape=jax.ShapeDtypeStruct((cents, cols), jnp.float32),
        compiler_params=params,
    )(in_vmem(own), in_vmem(mass), *[in_vmem(p) for p in parts])
    return new_centroids, log_totals.reshape(rows)


def solution(mesh):
    n_dp = mesh.shape["dp"]
    fine = Mesh(mesh.devices.reshape(n_dp, 8, 4, 2), ("x", "z", "y", "core"))
    cent = ("z", "y", "core")
    return jax.shard_map(
        functools.partial(shards, n_dp),
        mesh=fine,
        in_specs=(P("x", None), P(cent, None)),
        out_specs=(P(cent, "x"), P("x")),
        check_vma=False,
    )
```

```python
import functools
import math

import jax
import jax.numpy as jnp
from jax import lax
from jax.experimental import pallas as pl
from jax.experimental.pallas import tpu as pltpu
from jax.sharding import Mesh, PartitionSpec as P

SOFTNESS = 0.1
PRIOR = 4.0
LOG2E = math.log2(math.e)
LN2 = math.log(2.0)
ROWS = 256
LOADS = 2
LANES = 128
MASS_ROWS = 16
VMEM_LIMIT = 16 * 1024 * 1024
IN_VMEM = pl.BlockSpec(memory_space=pltpu.VMEM)
IN_HBM = pl.BlockSpec(memory_space=pltpu.HBM)


def in_vmem(x):
    return pltpu.with_memory_space_constraint(x, pltpu.VMEM)


def in_hbm(x):
    return pltpu.with_memory_space_constraint(x, pltpu.HBM)


def logits_kernel(scale, emb_hbm, cent_hbm, z_ref, lse_ref, emb_ref, prior_ref, cent_ref, half_sq, sems):
    rows = emb_ref.shape[0]
    cols = prior_ref.shape[1]
    cent_copy = pltpu.make_async_copy(cent_hbm, cent_ref, sems.at[LOADS])
    cent_copy.start()
    load = rows // LOADS
    copies = []
    for k in range(LOADS):
        part = pl.ds(k * load, load)
        copies.append(pltpu.make_async_copy(emb_hbm.at[part, :], emb_ref.at[part, :], sems.at[k]))
        copies[-1].start()
    cent_copy.wait()
    c = cent_ref[...].astype(jnp.float32)
    half_sq[...] = jnp.broadcast_to(0.5 * jnp.sum(c * c, axis=1, keepdims=True), half_sq.shape)
    first_col = pl.multiple_of(lax.axis_index("x") * cols, cols)
    prior_ref[...] = cent_ref[:, pl.ds(first_col, cols)]
    for r in range(0, rows, ROWS):
        if r % load == 0:
            copies[r // load].wait()
        inner = lax.dot_general(
            cent_ref[...], emb_ref[r : r + ROWS, :], (((1,), (1,)), ((), ())), preferred_element_type=jnp.float32
        )
        z = (inner - half_sq[:, :1]) * scale
        z_ref[:, r : r + ROWS] = z
        top = jnp.max(z, axis=0, keepdims=True)
        lse = top + jnp.log2(jnp.sum(jnp.exp2(z - top), axis=0, keepdims=True))
        for k in range(ROWS // LANES):
            lse_ref[pl.ds(r // LANES + k, 1), :] = lse[:, k * LANES : (k + 1) * LANES]


def merge(lse):
    top = jnp.max(lse, axis=0)
    return top + jnp.log2(jnp.sum(jnp.exp2(lse - top), axis=0))


def weights_kernel(shift, z_ref, every_ref, emb_ref, part_ref, w_ref, mass_ref, log_totals_ref):
    cents, rows = z_ref.shape
    totals = merge(every_ref[...])
    log_totals_ref[...] = totals * LN2
    mass = jnp.zeros((cents, LANES), jnp.float32)
    for k in range(rows // LANES):
        w = jnp.exp2(z_ref[:, k * LANES : (k + 1) * LANES] - totals[k : k + 1, :]).astype(jnp.bfloat16)
        w_ref[:, k * LANES : (k + 1) * LANES] = w
        mass = mass + w.astype(jnp.float32)
    cols = mass_ref.shape[1]
    mass = jnp.broadcast_to(jnp.sum(mass, axis=1, keepdims=True), (cents, LANES)).T
    half = MASS_ROWS // 2
    mass_ref[...] = jnp.concatenate([mass[:half, :cols], mass[:half, cols:]], axis=0).astype(jnp.bfloat16)
    part_product(shift, w_ref, emb_ref, mass_ref, part_ref)


def part_product(shift, w_ref, emb_ref, mass_ref, part_ref):
    cents = w_ref.shape[0]
    cols = mass_ref.shape[1]
    n_dp = emb_ref.shape[1] // cols
    first_col = pl.multiple_of(lax.rem(lax.axis_index("x") + shift, n_dp) * cols, cols)
    part_ref[:cents, :] = jnp.dot(
        w_ref[...], emb_ref[:, pl.ds(first_col, cols)], preferred_element_type=jnp.float32
    ).astype(jnp.bfloat16)
    part_ref[cents:, :] = mass_ref[...]


def parts_kernel(shifts, w_ref, emb_ref, mass_ref, *parts_refs):
    for shift, part_ref in zip(shifts, parts_refs):
        part_product(shift, w_ref, emb_ref, mass_ref, part_ref)


def own_kernel(w_ref, emb_ref, prior_ref, mass_ref, far_ref, out_ref, out_mass_ref):
    cents, cols = out_ref.shape
    first_col = pl.multiple_of(lax.axis_index("x") * cols, cols)
    own = jnp.dot(w_ref[...], emb_ref[:, pl.ds(first_col, cols)], preferred_element_type=jnp.float32)
    out_ref[...] = own + PRIOR * prior_ref[...].astype(jnp.float32) + far_ref[:cents, :].astype(jnp.float32)
    out_mass_ref[...] = PRIOR + mass_ref[...].astype(jnp.float32) + far_ref[cents:, :].astype(jnp.float32)


def update_kernel(own_ref, mass_ref, *refs):
    parts_refs, out_ref = refs[:-1], refs[-1]
    cents, cols = out_ref.shape
    total = own_ref[...]
    mass = mass_ref[...]
    for part_ref in parts_refs:
        total = total + part_ref[:cents, :].astype(jnp.float32)
        mass = mass + part_ref[cents:, :].astype(jnp.float32)
    half = MASS_ROWS // 2
    inv = 1.0 / jnp.concatenate([mass[:1, :], mass[half : half + 1, :]], axis=1)
    inv = jnp.broadcast_to(inv, (LANES, cents)).T
    for k in range(cols // LANES):
        out_ref[:, k * LANES : (k + 1) * LANES] = total[:, k * LANES : (k + 1) * LANES] * inv


def shards(n_dp, emb, cent):
    rows, width = emb.shape
    cents = cent.shape[0]
    cols = width // n_dp
    scale = 2.0 * LOG2E / (SOFTNESS * math.sqrt(width))
    params = pltpu.CompilerParams(vmem_limit_bytes=VMEM_LIMIT)
    z, lse, emb_vmem, prior = pl.pallas_call(
        functools.partial(logits_kernel, scale),
        in_specs=[IN_HBM] * 2,
        out_specs=[IN_VMEM] * 4,
        out_shape=[
            pltpu.VMEM((cents, rows), jnp.float32),
            pltpu.VMEM((rows // LANES, LANES), jnp.float32),
            pltpu.VMEM(emb.shape, emb.dtype),
            pltpu.VMEM((cents, cols), cent.dtype),
        ],
        scratch_shapes=[
            pltpu.VMEM(cent.shape, cent.dtype),
            pltpu.VMEM((cents, LANES), jnp.float32),
            pltpu.SemaphoreType.DMA((LOADS + 1,)),
        ],
        compiler_params=params,
    )(in_hbm(emb), in_hbm(cent))

    other = lax.ppermute(lse, "core", [(0, 1), (1, 0)])
    chip = merge(jnp.stack([lse, other]))
    chips = lax.axis_size("z") * lax.axis_size("y")
    every = lax.all_to_all(jnp.broadcast_to(chip, (chips,) + chip.shape), ("y", "z"), 0, 0)

    part = pltpu.VMEM((cents + MASS_ROWS, cols), jnp.bfloat16)
    first = n_dp // 2
    others = [k for k in range(1, n_dp) if k != first]
    far, w, mass, log_totals = pl.pallas_call(
        functools.partial(weights_kernel, first),
        in_specs=[IN_VMEM] * 3,
        out_specs=[IN_VMEM] * 4,
        out_shape=[
            part,
            pltpu.VMEM((cents, rows), jnp.bfloat16),
            pltpu.VMEM((MASS_ROWS, cols), jnp.bfloat16),
            jax.ShapeDtypeStruct(lse.shape, jnp.float32),
        ],
        compiler_params=params,
    )(in_vmem(z), in_vmem(every), in_vmem(emb_vmem))

    def send(p, shift):
        return lax.ppermute(p, "x", [(k, (k + shift) % n_dp) for k in range(n_dp)])

    near = pl.pallas_call(
        functools.partial(parts_kernel, others),
        in_specs=[IN_VMEM] * 3,
        out_specs=[IN_VMEM] * len(others),
        out_shape=[part] * len(others),
        compiler_params=params,
    )(in_vmem(w), in_vmem(emb_vmem), in_vmem(mass))
    own, own_mass = pl.pallas_call(
        own_kernel,
        in_specs=[IN_VMEM] * 5,
        out_specs=[IN_VMEM] * 2,
        out_shape=[pltpu.VMEM((cents, cols), jnp.float32), pltpu.VMEM((MASS_ROWS, cols), jnp.float32)],
        compiler_params=params,
    )(in_vmem(w), in_vmem(emb_vmem), in_vmem(prior), in_vmem(mass), in_vmem(send(far, first)))
    parts = [send(p, k) for k, p in zip(others, near)]
    new_centroids = pl.pallas_call(
        update_kernel,
        in_specs=[IN_VMEM] * (2 + len(parts)),
        out_specs=IN_VMEM,
        out_shape=jax.ShapeDtypeStruct((cents, cols), jnp.float32),
        compiler_params=params,
    )(in_vmem(own), in_vmem(own_mass), *[in_vmem(p) for p in parts])
    return new_centroids, log_totals.reshape(rows)


def solution(mesh):
    n_dp = mesh.shape["dp"]
    fine = Mesh(mesh.devices.reshape(n_dp, 8, 4, 2), ("x", "z", "y", "core"))
    cent = ("z", "y", "core")
    return jax.shard_map(
        functools.partial(shards, n_dp),
        mesh=fine,
        in_specs=(P("x", None), P(cent, None)),
        out_specs=(P(cent, "x"), P("x")),
        check_vma=False,
    )
```

```python
import functools
import math

import jax
import jax.numpy as jnp
from jax import lax
from jax.experimental import pallas as pl
from jax.experimental.pallas import tpu as pltpu
from jax.sharding import Mesh, PartitionSpec as P

SOFTNESS = 0.1
PRIOR = 4.0
LOG2E = math.log2(math.e)
LN2 = math.log(2.0)
ROWS = 256
LOADS = 2
LANES = 128
MASS_ROWS = 16
VMEM_LIMIT = 16 * 1024 * 1024
IN_VMEM = pl.BlockSpec(memory_space=pltpu.VMEM)
IN_HBM = pl.BlockSpec(memory_space=pltpu.HBM)


def in_vmem(x):
    return pltpu.with_memory_space_constraint(x, pltpu.VMEM)


def in_hbm(x):
    return pltpu.with_memory_space_constraint(x, pltpu.HBM)


def logits_kernel(scale, emb_hbm, cent_hbm, z_ref, lse_ref, emb_ref, prior_ref, cent_ref, half_sq, sems):
    rows = emb_ref.shape[0]
    cols = prior_ref.shape[1]
    cent_copy = pltpu.make_async_copy(cent_hbm, cent_ref, sems.at[LOADS])
    cent_copy.start()
    load = rows // LOADS
    copies = []
    for k in range(LOADS):
        part = pl.ds(k * load, load)
        copies.append(pltpu.make_async_copy(emb_hbm.at[part, :], emb_ref.at[part, :], sems.at[k]))
        copies[-1].start()
    cent_copy.wait()
    c = cent_ref[...].astype(jnp.float32)
    half_sq[...] = jnp.broadcast_to(0.5 * jnp.sum(c * c, axis=1, keepdims=True), half_sq.shape)
    first_col = pl.multiple_of(lax.axis_index("x") * cols, cols)
    prior_ref[...] = cent_ref[:, pl.ds(first_col, cols)]
    for r in range(0, rows, ROWS):
        if r % load == 0:
            copies[r // load].wait()
        inner = lax.dot_general(
            cent_ref[...], emb_ref[r : r + ROWS, :], (((1,), (1,)), ((), ())), preferred_element_type=jnp.float32
        )
        z = (inner - half_sq[:, :1]) * scale
        z_ref[:, r : r + ROWS] = z
        top = jnp.max(z, axis=0, keepdims=True)
        lse = top + jnp.log2(jnp.sum(jnp.exp2(z - top), axis=0, keepdims=True))
        for k in range(ROWS // LANES):
            lse_ref[pl.ds(r // LANES + k, 1), :] = lse[:, k * LANES : (k + 1) * LANES]


def merge(lse):
    top = jnp.max(lse, axis=0)
    return top + jnp.log2(jnp.sum(jnp.exp2(lse - top), axis=0))


def weights_kernel(shift, z_ref, every_ref, emb_ref, part_ref, w_ref, mass_ref, log_totals_ref):
    cents, rows = z_ref.shape
    totals = merge(every_ref[...])
    log_totals_ref[...] = totals * LN2
    mass = jnp.zeros((cents, LANES), jnp.float32)
    for k in range(rows // LANES):
        w = jnp.exp2(z_ref[:, k * LANES : (k + 1) * LANES] - totals[k : k + 1, :])
        w_ref[:, k * LANES : (k + 1) * LANES] = w.astype(jnp.bfloat16)
        mass = mass + w
    cols = mass_ref.shape[1]
    mass = jnp.broadcast_to(jnp.sum(mass, axis=1, keepdims=True), (cents, LANES)).T
    half = MASS_ROWS // 2
    mass_ref[...] = jnp.concatenate([mass[:half, :cols], mass[:half, cols:]], axis=0).astype(jnp.bfloat16)
    part_product(shift, w_ref, emb_ref, mass_ref, part_ref)


def part_product(shift, w_ref, emb_ref, mass_ref, part_ref):
    cents = w_ref.shape[0]
    cols = mass_ref.shape[1]
    n_dp = emb_ref.shape[1] // cols
    first_col = pl.multiple_of(lax.rem(lax.axis_index("x") + shift, n_dp) * cols, cols)
    part_ref[:cents, :] = jnp.dot(
        w_ref[...], emb_ref[:, pl.ds(first_col, cols)], preferred_element_type=jnp.float32
    ).astype(jnp.bfloat16)
    part_ref[cents:, :] = mass_ref[...]


def parts_kernel(shifts, w_ref, emb_ref, mass_ref, *parts_refs):
    for shift, part_ref in zip(shifts, parts_refs):
        part_product(shift, w_ref, emb_ref, mass_ref, part_ref)


def own_kernel(w_ref, emb_ref, prior_ref, mass_ref, far_ref, out_ref, out_mass_ref):
    cents, cols = out_ref.shape
    first_col = pl.multiple_of(lax.axis_index("x") * cols, cols)
    own = jnp.dot(w_ref[...], emb_ref[:, pl.ds(first_col, cols)], preferred_element_type=jnp.float32)
    out_ref[...] = own + PRIOR * prior_ref[...].astype(jnp.float32) + far_ref[:cents, :].astype(jnp.float32)
    out_mass_ref[...] = PRIOR + mass_ref[...].astype(jnp.float32) + far_ref[cents:, :].astype(jnp.float32)


def update_kernel(own_ref, mass_ref, *refs):
    parts_refs, out_ref = refs[:-1], refs[-1]
    cents, cols = out_ref.shape
    total = own_ref[...]
    mass = mass_ref[...]
    for part_ref in parts_refs:
        total = total + part_ref[:cents, :].astype(jnp.float32)
        mass = mass + part_ref[cents:, :].astype(jnp.float32)
    half = MASS_ROWS // 2
    inv = 1.0 / jnp.concatenate([mass[:1, :], mass[half : half + 1, :]], axis=1)
    inv = jnp.broadcast_to(inv, (LANES, cents)).T
    for k in range(cols // LANES):
        out_ref[:, k * LANES : (k + 1) * LANES] = total[:, k * LANES : (k + 1) * LANES] * inv


def shards(n_dp, emb, cent):
    rows, width = emb.shape
    cents = cent.shape[0]
    cols = width // n_dp
    scale = 2.0 * LOG2E / (SOFTNESS * math.sqrt(width))
    params = pltpu.CompilerParams(vmem_limit_bytes=VMEM_LIMIT)
    z, lse, emb_vmem, prior = pl.pallas_call(
        functools.partial(logits_kernel, scale),
        in_specs=[IN_HBM] * 2,
        out_specs=[IN_VMEM] * 4,
        out_shape=[
            pltpu.VMEM((cents, rows), jnp.float32),
            pltpu.VMEM((rows // LANES, LANES), jnp.float32),
            pltpu.VMEM(emb.shape, emb.dtype),
            pltpu.VMEM((cents, cols), cent.dtype),
        ],
        scratch_shapes=[
            pltpu.VMEM(cent.shape, cent.dtype),
            pltpu.VMEM((cents, LANES), jnp.float32),
            pltpu.SemaphoreType.DMA((LOADS + 1,)),
        ],
        compiler_params=params,
    )(in_hbm(emb), in_hbm(cent))

    other = lax.ppermute(lse, "core", [(0, 1), (1, 0)])
    chip = merge(jnp.stack([lse, other]))
    chips = lax.axis_size("z") * lax.axis_size("y")
    every = lax.all_to_all(jnp.broadcast_to(chip, (chips,) + chip.shape), ("y", "z"), 0, 0)

    part = pltpu.VMEM((cents + MASS_ROWS, cols), jnp.bfloat16)
    first = n_dp // 2
    others = [k for k in range(1, n_dp) if k != first]
    far, w, mass, log_totals = pl.pallas_call(
        functools.partial(weights_kernel, first),
        in_specs=[IN_VMEM] * 3,
        out_specs=[IN_VMEM] * 4,
        out_shape=[
            part,
            pltpu.VMEM((cents, rows), jnp.bfloat16),
            pltpu.VMEM((MASS_ROWS, cols), jnp.bfloat16),
            jax.ShapeDtypeStruct(lse.shape, jnp.float32),
        ],
        compiler_params=params,
    )(in_vmem(z), in_vmem(every), in_vmem(emb_vmem))

    def send(p, shift):
        return lax.ppermute(p, "x", [(k, (k + shift) % n_dp) for k in range(n_dp)])

    near = pl.pallas_call(
        functools.partial(parts_kernel, others),
        in_specs=[IN_VMEM] * 3,
        out_specs=[IN_VMEM] * len(others),
        out_shape=[part] * len(others),
        compiler_params=params,
    )(in_vmem(w), in_vmem(emb_vmem), in_vmem(mass))
    own, own_mass = pl.pallas_call(
        own_kernel,
        in_specs=[IN_VMEM] * 5,
        out_specs=[IN_VMEM] * 2,
        out_shape=[pltpu.VMEM((cents, cols), jnp.float32), pltpu.VMEM((MASS_ROWS, cols), jnp.float32)],
        compiler_params=params,
    )(in_vmem(w), in_vmem(emb_vmem), in_vmem(prior), in_vmem(mass), in_vmem(send(far, first)))
    parts = [send(p, k) for k, p in zip(others, near)]
    new_centroids = pl.pallas_call(
        update_kernel,
        in_specs=[IN_VMEM] * (2 + len(parts)),
        out_specs=IN_VMEM,
        out_shape=jax.ShapeDtypeStruct((cents, cols), jnp.float32),
        compiler_params=params,
    )(in_vmem(own), in_vmem(own_mass), *[in_vmem(p) for p in parts])
    return new_centroids, log_totals.reshape(rows)


def solution(mesh):
    n_dp = mesh.shape["dp"]
    fine = Mesh(mesh.devices.reshape(n_dp, 8, 4, 2), ("x", "z", "y", "core"))
    cent = ("z", "y", "core")
    return jax.shard_map(
        functools.partial(shards, n_dp),
        mesh=fine,
        in_specs=(P("x", None), P(cent, None)),
        out_specs=(P(cent, "x"), P("x")),
        check_vma=False,
    )
```

```python
import functools
import math

import jax
import jax.numpy as jnp
from jax import lax
from jax.experimental import pallas as pl
from jax.experimental.pallas import tpu as pltpu
from jax.sharding import Mesh, PartitionSpec as P

SOFTNESS = 0.1
PRIOR = 4.0
LOG2E = math.log2(math.e)
LN2 = math.log(2.0)
ROWS = 256
FIRST_LOAD = 512
LANES = 128
EXCHANGE = ("y", "z_lo", "z_hi")
MASS_ROWS = 16
VMEM_LIMIT = 16 * 1024 * 1024
IN_VMEM = pl.BlockSpec(memory_space=pltpu.VMEM)
IN_HBM = pl.BlockSpec(memory_space=pltpu.HBM)


def in_vmem(x):
    return pltpu.with_memory_space_constraint(x, pltpu.VMEM)


def in_hbm(x):
    return pltpu.with_memory_space_constraint(x, pltpu.HBM)


def logits_kernel(scale, emb_hbm, cent_hbm, z_ref, lse_ref, emb_ref, prior_ref, cent_ref, half_sq, sems):
    rows = emb_ref.shape[0]
    cols = prior_ref.shape[1]
    cent_copy = pltpu.make_async_copy(cent_hbm, cent_ref, sems.at[0])
    cent_copy.start()
    copies = {}
    for start, end in ((0, FIRST_LOAD), (FIRST_LOAD, rows)):
        part = pl.ds(start, end - start)
        sem = sems.at[1 + len(copies)]
        copies[start] = pltpu.make_async_copy(emb_hbm.at[part, :], emb_ref.at[part, :], sem)
        copies[start].start()
    cent_copy.wait()
    c = cent_ref[...].astype(jnp.float32)
    half_sq[...] = jnp.broadcast_to(0.5 * jnp.sum(c * c, axis=1, keepdims=True), half_sq.shape)
    first_col = pl.multiple_of(lax.axis_index("x") * cols, cols)
    prior_ref[...] = cent_ref[:, pl.ds(first_col, cols)]
    for r in range(0, rows, ROWS):
        if r in copies:
            copies[r].wait()
        inner = lax.dot_general(
            cent_ref[...], emb_ref[r : r + ROWS, :], (((1,), (1,)), ((), ())), preferred_element_type=jnp.float32
        )
        z = (inner - half_sq[:, :1]) * scale
        z_ref[:, r : r + ROWS] = z
        top = jnp.max(z, axis=0, keepdims=True)
        lse = top + jnp.log2(jnp.sum(jnp.exp2(z - top), axis=0, keepdims=True))
        for k in range(ROWS // LANES):
            lse_ref[pl.ds(r // LANES + k, 1), :] = lse[:, k * LANES : (k + 1) * LANES]


def merge(lse):
    top = jnp.max(lse, axis=0)
    return top + jnp.log2(jnp.sum(jnp.exp2(lse - top), axis=0))


def weights_kernel(shift, z_ref, every_ref, emb_ref, part_ref, w_ref, mass_ref, log_totals_ref):
    cents, rows = z_ref.shape
    totals = merge(every_ref[...])
    log_totals_ref[...] = totals * LN2
    mass = jnp.zeros((cents, LANES), jnp.float32)
    for k in range(rows // LANES):
        w = jnp.exp2(z_ref[:, k * LANES : (k + 1) * LANES] - totals[k : k + 1, :])
        w_ref[:, k * LANES : (k + 1) * LANES] = w.astype(jnp.bfloat16)
        mass = mass + w
    cols = mass_ref.shape[1]
    mass = jnp.broadcast_to(jnp.sum(mass, axis=1, keepdims=True), (cents, LANES)).T
    half = MASS_ROWS // 2
    mass_ref[...] = jnp.concatenate([mass[:half, :cols], mass[:half, cols:]], axis=0).astype(jnp.bfloat16)
    part_product(shift, w_ref, emb_ref, mass_ref, part_ref)


def part_product(shift, w_ref, emb_ref, mass_ref, part_ref):
    cents = w_ref.shape[0]
    cols = mass_ref.shape[1]
    n_dp = emb_ref.shape[1] // cols
    first_col = pl.multiple_of(lax.rem(lax.axis_index("x") + shift, n_dp) * cols, cols)
    part_ref[:cents, :] = jnp.dot(
        w_ref[...], emb_ref[:, pl.ds(first_col, cols)], preferred_element_type=jnp.float32
    ).astype(jnp.bfloat16)
    part_ref[cents:, :] = mass_ref[...]


def parts_kernel(shifts, w_ref, emb_ref, mass_ref, *parts_refs):
    for shift, part_ref in zip(shifts, parts_refs):
        part_product(shift, w_ref, emb_ref, mass_ref, part_ref)


def own_kernel(w_ref, emb_ref, prior_ref, mass_ref, far_ref, out_ref, out_mass_ref):
    cents, cols = out_ref.shape
    first_col = pl.multiple_of(lax.axis_index("x") * cols, cols)
    own = jnp.dot(w_ref[...], emb_ref[:, pl.ds(first_col, cols)], preferred_element_type=jnp.float32)
    out_ref[...] = own + PRIOR * prior_ref[...].astype(jnp.float32) + far_ref[:cents, :].astype(jnp.float32)
    out_mass_ref[...] = PRIOR + mass_ref[...].astype(jnp.float32) + far_ref[cents:, :].astype(jnp.float32)


def update_kernel(own_ref, mass_ref, *refs):
    parts_refs, out_ref = refs[:-1], refs[-1]
    cents, cols = out_ref.shape
    total = own_ref[...]
    mass = mass_ref[...]
    for part_ref in parts_refs:
        total = total + part_ref[:cents, :].astype(jnp.float32)
        mass = mass + part_ref[cents:, :].astype(jnp.float32)
    half = MASS_ROWS // 2
    inv = 1.0 / jnp.concatenate([mass[:1, :], mass[half : half + 1, :]], axis=1)
    inv = jnp.broadcast_to(inv, (LANES, cents)).T
    for k in range(cols // LANES):
        out_ref[:, k * LANES : (k + 1) * LANES] = total[:, k * LANES : (k + 1) * LANES] * inv


def shards(n_dp, emb, cent):
    rows, width = emb.shape
    cents = cent.shape[0]
    cols = width // n_dp
    scale = 2.0 * LOG2E / (SOFTNESS * math.sqrt(width))
    params = pltpu.CompilerParams(vmem_limit_bytes=VMEM_LIMIT)
    z, lse, emb_vmem, prior = pl.pallas_call(
        functools.partial(logits_kernel, scale),
        in_specs=[IN_HBM] * 2,
        out_specs=[IN_VMEM] * 4,
        out_shape=[
            pltpu.VMEM((cents, rows), jnp.float32),
            pltpu.VMEM((rows // LANES, LANES), jnp.float32),
            pltpu.VMEM(emb.shape, emb.dtype),
            pltpu.VMEM((cents, cols), cent.dtype),
        ],
        scratch_shapes=[
            pltpu.VMEM(cent.shape, cent.dtype),
            pltpu.VMEM((cents, LANES), jnp.float32),
            pltpu.SemaphoreType.DMA((3,)),
        ],
        compiler_params=params,
    )(in_hbm(emb), in_hbm(cent))

    other = lax.ppermute(lse, "core", [(0, 1), (1, 0)])
    chip = merge(jnp.stack([lse, other]))
    chips = math.prod(lax.axis_size(axis) for axis in EXCHANGE)
    every = lax.all_to_all(jnp.broadcast_to(chip, (chips,) + chip.shape), EXCHANGE, 0, 0)

    part = pltpu.VMEM((cents + MASS_ROWS, cols), jnp.bfloat16)
    first = n_dp // 2
    others = [k for k in range(1, n_dp) if k != first]
    far, w, mass, log_totals = pl.pallas_call(
        functools.partial(weights_kernel, first),
        in_specs=[IN_VMEM] * 3,
        out_specs=[IN_VMEM] * 4,
        out_shape=[
            part,
            pltpu.VMEM((cents, rows), jnp.bfloat16),
            pltpu.VMEM((MASS_ROWS, cols), jnp.bfloat16),
            jax.ShapeDtypeStruct(lse.shape, jnp.float32),
        ],
        compiler_params=params,
    )(in_vmem(z), in_vmem(every), in_vmem(emb_vmem))

    def send(p, shift):
        return lax.ppermute(p, "x", [(k, (k + shift) % n_dp) for k in range(n_dp)])

    near = pl.pallas_call(
        functools.partial(parts_kernel, others),
        in_specs=[IN_VMEM] * 3,
        out_specs=[IN_VMEM] * len(others),
        out_shape=[part] * len(others),
        compiler_params=params,
    )(in_vmem(w), in_vmem(emb_vmem), in_vmem(mass))
    own, own_mass = pl.pallas_call(
        own_kernel,
        in_specs=[IN_VMEM] * 5,
        out_specs=[IN_VMEM] * 2,
        out_shape=[pltpu.VMEM((cents, cols), jnp.float32), pltpu.VMEM((MASS_ROWS, cols), jnp.float32)],
        compiler_params=params,
    )(in_vmem(w), in_vmem(emb_vmem), in_vmem(prior), in_vmem(mass), in_vmem(send(far, first)))
    parts = [send(p, k) for k, p in zip(others, near)]
    new_centroids = pl.pallas_call(
        update_kernel,
        in_specs=[IN_VMEM] * (2 + len(parts)),
        out_specs=IN_VMEM,
        out_shape=jax.ShapeDtypeStruct((cents, cols), jnp.float32),
        compiler_params=params,
    )(in_vmem(own), in_vmem(own_mass), *[in_vmem(p) for p in parts])
    return new_centroids, log_totals.reshape(rows)


def solution(mesh):
    n_dp = mesh.shape["dp"]
    fine = Mesh(mesh.devices.reshape(n_dp, 4, 2, 4, 2), ("x", "z_hi", "z_lo", "y", "core"))
    cent = ("z_hi", "z_lo", "y", "core")
    return jax.shard_map(
        functools.partial(shards, n_dp),
        mesh=fine,
        in_specs=(P("x", None), P(cent, None)),
        out_specs=(P(cent, "x"), P("x")),
        check_vma=False,
    )
```

```python
import functools
import math

import jax
import jax.numpy as jnp
from jax import lax
from jax.experimental import pallas as pl
from jax.experimental.pallas import tpu as pltpu
from jax.sharding import Mesh, PartitionSpec as P

SOFTNESS = 0.1
PRIOR = 4.0
LOG2E = math.log2(math.e)
LN2 = math.log(2.0)
ROWS = 256
FIRST_LOAD = 512
LANES = 128
EXCHANGE = ("y", "z_lo", "z_hi")
MASS_ROWS = 16
VMEM_LIMIT = 16 * 1024 * 1024
IN_VMEM = pl.BlockSpec(memory_space=pltpu.VMEM)
IN_HBM = pl.BlockSpec(memory_space=pltpu.HBM)


def in_vmem(x):
    return pltpu.with_memory_space_constraint(x, pltpu.VMEM)


def in_hbm(x):
    return pltpu.with_memory_space_constraint(x, pltpu.HBM)


def logits_kernel(scale, emb_hbm, cent_hbm, p_ref, top_ref, lse_ref, emb_ref, prior_ref, cent_ref, half_sq, sems):
    rows = emb_ref.shape[0]
    cols = prior_ref.shape[1]
    cent_copy = pltpu.make_async_copy(cent_hbm, cent_ref, sems.at[0])
    cent_copy.start()
    copies = {}
    for start, end in ((0, FIRST_LOAD), (FIRST_LOAD, rows)):
        part = pl.ds(start, end - start)
        sem = sems.at[1 + len(copies)]
        copies[start] = pltpu.make_async_copy(emb_hbm.at[part, :], emb_ref.at[part, :], sem)
        copies[start].start()
    cent_copy.wait()
    c = cent_ref[...].astype(jnp.float32)
    half_sq[...] = jnp.broadcast_to(0.5 * jnp.sum(c * c, axis=1, keepdims=True), half_sq.shape)
    first_col = pl.multiple_of(lax.axis_index("x") * cols, cols)
    prior_ref[...] = cent_ref[:, pl.ds(first_col, cols)]
    for r in range(0, rows, ROWS):
        if r in copies:
            copies[r].wait()
        inner = lax.dot_general(
            cent_ref[...], emb_ref[r : r + ROWS, :], (((1,), (1,)), ((), ())), preferred_element_type=jnp.float32
        )
        z = (inner - half_sq[:, :1]) * scale
        top = jnp.max(z, axis=0, keepdims=True)
        p = jnp.exp2(z - top)
        p_ref[:, r : r + ROWS] = p
        lse = top + jnp.log2(jnp.sum(p, axis=0, keepdims=True))
        for k in range(ROWS // LANES):
            top_ref[pl.ds(r // LANES + k, 1), :] = top[:, k * LANES : (k + 1) * LANES]
            lse_ref[pl.ds(r // LANES + k, 1), :] = lse[:, k * LANES : (k + 1) * LANES]


def merge(lse):
    top = jnp.max(lse, axis=0)
    return top + jnp.log2(jnp.sum(jnp.exp2(lse - top), axis=0))


def weights_kernel(shift, p_ref, top_ref, every_ref, emb_ref, part_ref, w_ref, mass_ref, log_totals_ref):
    cents, rows = p_ref.shape
    cols = mass_ref.shape[1]
    totals = merge(every_ref[...])
    log_totals_ref[...] = totals * LN2
    factor = jnp.exp2(top_ref[...] - totals)
    mass = jnp.zeros((cents, LANES), jnp.float32)
    for k in range(rows // LANES):
        w = p_ref[:, k * LANES : (k + 1) * LANES] * factor[k : k + 1, :]
        w_ref[:, k * LANES : (k + 1) * LANES] = w.astype(jnp.bfloat16)
        mass = mass + w
    part_ref[:cents, :] = part_product(shift, w_ref, emb_ref).astype(jnp.bfloat16)
    mass = jnp.broadcast_to(jnp.sum(mass, axis=1, keepdims=True), (cents, LANES)).T
    half = MASS_ROWS // 2
    mass = jnp.concatenate([mass[:half, :cols], mass[:half, cols:]], axis=0).astype(jnp.bfloat16)
    mass_ref[...] = mass
    part_ref[cents:, :] = mass


def part_product(shift, w_ref, emb_ref):
    n_dp = lax.axis_size("x")
    cols = emb_ref.shape[1] // n_dp
    first_col = pl.multiple_of(lax.rem(lax.axis_index("x") + shift, n_dp) * cols, cols)
    return jnp.dot(w_ref[...], emb_ref[:, pl.ds(first_col, cols)], preferred_element_type=jnp.float32)


def parts_kernel(shifts, w_ref, emb_ref, mass_ref, *parts_refs):
    cents = w_ref.shape[0]
    for shift, part_ref in zip(shifts, parts_refs):
        part_ref[:cents, :] = part_product(shift, w_ref, emb_ref).astype(jnp.bfloat16)
        part_ref[cents:, :] = mass_ref[...]


def own_kernel(w_ref, emb_ref, prior_ref, mass_ref, far_ref, out_ref, out_mass_ref):
    cents = out_ref.shape[0]
    own = part_product(0, w_ref, emb_ref)
    out_ref[...] = own + PRIOR * prior_ref[...].astype(jnp.float32) + far_ref[:cents, :].astype(jnp.float32)
    out_mass_ref[...] = PRIOR + mass_ref[...].astype(jnp.float32) + far_ref[cents:, :].astype(jnp.float32)


def update_kernel(own_ref, mass_ref, *refs):
    parts_refs, out_ref = refs[:-1], refs[-1]
    cents, cols = out_ref.shape
    total = own_ref[...]
    mass = mass_ref[...]
    for part_ref in parts_refs:
        total = total + part_ref[:cents, :].astype(jnp.float32)
        mass = mass + part_ref[cents:, :].astype(jnp.float32)
    half = MASS_ROWS // 2
    inv = 1.0 / jnp.concatenate([mass[:1, :], mass[half : half + 1, :]], axis=1)
    inv = jnp.broadcast_to(inv, (LANES, cents)).T
    for k in range(cols // LANES):
        out_ref[:, k * LANES : (k + 1) * LANES] = total[:, k * LANES : (k + 1) * LANES] * inv


def shards(n_dp, emb, cent):
    rows, width = emb.shape
    cents = cent.shape[0]
    cols = width // n_dp
    scale = 2.0 * LOG2E / (SOFTNESS * math.sqrt(width))
    params = pltpu.CompilerParams(vmem_limit_bytes=VMEM_LIMIT)
    p, top, lse, emb_vmem, prior = pl.pallas_call(
        functools.partial(logits_kernel, scale),
        in_specs=[IN_HBM] * 2,
        out_specs=[IN_VMEM] * 5,
        out_shape=[
            pltpu.VMEM((cents, rows), jnp.float32),
            pltpu.VMEM((rows // LANES, LANES), jnp.float32),
            pltpu.VMEM((rows // LANES, LANES), jnp.float32),
            pltpu.VMEM(emb.shape, emb.dtype),
            pltpu.VMEM((cents, cols), cent.dtype),
        ],
        scratch_shapes=[
            pltpu.VMEM(cent.shape, cent.dtype),
            pltpu.VMEM((cents, LANES), jnp.float32),
            pltpu.SemaphoreType.DMA((3,)),
        ],
        compiler_params=params,
    )(in_hbm(emb), in_hbm(cent))

    other = lax.ppermute(lse, "core", [(0, 1), (1, 0)])
    chip = merge(jnp.stack([lse, other]))
    chips = math.prod(lax.axis_size(axis) for axis in EXCHANGE)
    every = lax.all_to_all(jnp.broadcast_to(chip, (chips,) + chip.shape), EXCHANGE, 0, 0)

    part = pltpu.VMEM((cents + MASS_ROWS, cols), jnp.bfloat16)
    first = n_dp // 2
    others = [k for k in range(1, n_dp) if k != first]
    far, w, mass, log_totals = pl.pallas_call(
        functools.partial(weights_kernel, first),
        in_specs=[IN_VMEM] * 4,
        out_specs=[IN_VMEM] * 4,
        out_shape=[
            part,
            pltpu.VMEM((cents, rows), jnp.bfloat16),
            pltpu.VMEM((MASS_ROWS, cols), jnp.bfloat16),
            jax.ShapeDtypeStruct(lse.shape, jnp.float32),
        ],
        compiler_params=params,
    )(in_vmem(p), in_vmem(top), in_vmem(every), in_vmem(emb_vmem))

    def send(p, shift):
        return lax.ppermute(p, "x", [(k, (k + shift) % n_dp) for k in range(n_dp)])

    near = pl.pallas_call(
        functools.partial(parts_kernel, others),
        in_specs=[IN_VMEM] * 3,
        out_specs=[IN_VMEM] * len(others),
        out_shape=[part] * len(others),
        compiler_params=params,
    )(in_vmem(w), in_vmem(emb_vmem), in_vmem(mass))
    own, own_mass = pl.pallas_call(
        own_kernel,
        in_specs=[IN_VMEM] * 5,
        out_specs=[IN_VMEM] * 2,
        out_shape=[pltpu.VMEM((cents, cols), jnp.float32), pltpu.VMEM((MASS_ROWS, cols), jnp.float32)],
        compiler_params=params,
    )(in_vmem(w), in_vmem(emb_vmem), in_vmem(prior), in_vmem(mass), in_vmem(send(far, first)))
    parts = [send(p, k) for k, p in zip(others, near)]
    new_centroids = pl.pallas_call(
        update_kernel,
        in_specs=[IN_VMEM] * (2 + len(parts)),
        out_specs=IN_VMEM,
        out_shape=jax.ShapeDtypeStruct((cents, cols), jnp.float32),
        compiler_params=params,
    )(in_vmem(own), in_vmem(own_mass), *[in_vmem(p) for p in parts])
    return new_centroids, log_totals.reshape(rows)


def solution(mesh):
    n_dp = mesh.shape["dp"]
    fine = Mesh(mesh.devices.reshape(n_dp, 4, 2, 4, 2), ("x", "z_hi", "z_lo", "y", "core"))
    cent = ("z_hi", "z_lo", "y", "core")
    return jax.shard_map(
        functools.partial(shards, n_dp),
        mesh=fine,
        in_specs=(P("x", None), P(cent, None)),
        out_specs=(P(cent, "x"), P("x")),
        check_vma=False,
    )
```

```python
import functools
import math

import jax
import jax.numpy as jnp
from jax import lax
from jax.experimental import pallas as pl
from jax.experimental.pallas import tpu as pltpu
from jax.sharding import Mesh, PartitionSpec as P

SOFTNESS = 0.1
PRIOR = 4.0
LOG2E = math.log2(math.e)
LN2 = math.log(2.0)
ROWS = 512
FIRST_LOAD = 512
LANES = 128
EXCHANGE = ("y", "z_lo", "z_hi")
MASS_ROWS = 16
VMEM_LIMIT = 16 * 1024 * 1024
IN_VMEM = pl.BlockSpec(memory_space=pltpu.VMEM)
IN_HBM = pl.BlockSpec(memory_space=pltpu.HBM)


def in_vmem(x):
    return pltpu.with_memory_space_constraint(x, pltpu.VMEM)


def in_hbm(x):
    return pltpu.with_memory_space_constraint(x, pltpu.HBM)


def logits_kernel(scale, emb_hbm, cent_hbm, p_ref, top_ref, lse_ref, emb_ref, prior_ref, cent_ref, half_sq, sems):
    rows = emb_ref.shape[0]
    cols = prior_ref.shape[1]
    cent_copy = pltpu.make_async_copy(cent_hbm, cent_ref, sems.at[0])
    cent_copy.start()
    copies = {}
    for start, end in ((0, FIRST_LOAD), (FIRST_LOAD, rows)):
        part = pl.ds(start, end - start)
        sem = sems.at[1 + len(copies)]
        copies[start] = pltpu.make_async_copy(emb_hbm.at[part, :], emb_ref.at[part, :], sem)
        copies[start].start()
    cent_copy.wait()
    c = cent_ref[...].astype(jnp.float32)
    half_sq[...] = jnp.broadcast_to(0.5 * jnp.sum(c * c, axis=1, keepdims=True), half_sq.shape)
    first_col = pl.multiple_of(lax.axis_index("x") * cols, cols)
    prior_ref[...] = cent_ref[:, pl.ds(first_col, cols)]
    for r in range(0, rows, ROWS):
        if r in copies:
            copies[r].wait()
        inner = lax.dot_general(
            cent_ref[...], emb_ref[r : r + ROWS, :], (((1,), (1,)), ((), ())), preferred_element_type=jnp.float32
        )
        z = (inner - half_sq[:, :1]) * scale
        top = jnp.max(z, axis=0, keepdims=True)
        p = jnp.exp2(z - top)
        p_ref[:, r : r + ROWS] = p
        lse = top + jnp.log2(jnp.sum(p, axis=0, keepdims=True))
        for k in range(ROWS // LANES):
            top_ref[pl.ds(r // LANES + k, 1), :] = top[:, k * LANES : (k + 1) * LANES]
            lse_ref[pl.ds(r // LANES + k, 1), :] = lse[:, k * LANES : (k + 1) * LANES]


def merge(lse):
    top = jnp.max(lse, axis=0)
    return top + jnp.log2(jnp.sum(jnp.exp2(lse - top), axis=0))


def weights_kernel(shift, p_ref, top_ref, every_ref, emb_ref, part_ref, w_ref, mass_ref, log_totals_ref):
    cents, rows = p_ref.shape
    cols = mass_ref.shape[1]
    totals = merge(every_ref[...])
    log_totals_ref[...] = totals * LN2
    factor = jnp.exp2(top_ref[...] - totals)
    mass = jnp.zeros((cents, LANES), jnp.float32)
    for k in range(rows // LANES):
        w = p_ref[:, k * LANES : (k + 1) * LANES] * factor[k : k + 1, :]
        w_ref[:, k * LANES : (k + 1) * LANES] = w.astype(jnp.bfloat16)
        mass = mass + w
    part_ref[:cents, :] = part_product(shift, w_ref, emb_ref).astype(jnp.bfloat16)
    mass = jnp.broadcast_to(jnp.sum(mass, axis=1, keepdims=True), (cents, LANES)).T
    half = MASS_ROWS // 2
    mass = jnp.concatenate([mass[:half, :cols], mass[:half, cols:]], axis=0).astype(jnp.bfloat16)
    mass_ref[...] = mass
    part_ref[cents:, :] = mass


def part_product(shift, w_ref, emb_ref):
    n_dp = lax.axis_size("x")
    cols = emb_ref.shape[1] // n_dp
    first_col = pl.multiple_of(lax.rem(lax.axis_index("x") + shift, n_dp) * cols, cols)
    return jnp.dot(w_ref[...], emb_ref[:, pl.ds(first_col, cols)], preferred_element_type=jnp.float32)


def parts_kernel(shifts, w_ref, emb_ref, mass_ref, *parts_refs):
    cents = w_ref.shape[0]
    for shift, part_ref in zip(shifts, parts_refs):
        part_ref[:cents, :] = part_product(shift, w_ref, emb_ref).astype(jnp.bfloat16)
        part_ref[cents:, :] = mass_ref[...]


def own_kernel(w_ref, emb_ref, prior_ref, mass_ref, far_ref, out_ref, out_mass_ref):
    cents = out_ref.shape[0]
    own = part_product(0, w_ref, emb_ref)
    out_ref[...] = own + PRIOR * prior_ref[...].astype(jnp.float32) + far_ref[:cents, :].astype(jnp.float32)
    out_mass_ref[...] = PRIOR + mass_ref[...].astype(jnp.float32) + far_ref[cents:, :].astype(jnp.float32)


def update_kernel(own_ref, mass_ref, *refs):
    parts_refs, out_ref = refs[:-1], refs[-1]
    cents, cols = out_ref.shape
    total = own_ref[...]
    mass = mass_ref[...]
    for part_ref in parts_refs:
        total = total + part_ref[:cents, :].astype(jnp.float32)
        mass = mass + part_ref[cents:, :].astype(jnp.float32)
    half = MASS_ROWS // 2
    inv = 1.0 / jnp.concatenate([mass[:1, :], mass[half : half + 1, :]], axis=1)
    inv = jnp.broadcast_to(inv, (LANES, cents)).T
    for k in range(cols // LANES):
        out_ref[:, k * LANES : (k + 1) * LANES] = total[:, k * LANES : (k + 1) * LANES] * inv


def shards(n_dp, emb, cent):
    rows, width = emb.shape
    cents = cent.shape[0]
    cols = width // n_dp
    scale = 2.0 * LOG2E / (SOFTNESS * math.sqrt(width))
    params = pltpu.CompilerParams(vmem_limit_bytes=VMEM_LIMIT)
    p, top, lse, emb_vmem, prior = pl.pallas_call(
        functools.partial(logits_kernel, scale),
        in_specs=[IN_HBM] * 2,
        out_specs=[IN_VMEM] * 5,
        out_shape=[
            pltpu.VMEM((cents, rows), jnp.float32),
            pltpu.VMEM((rows // LANES, LANES), jnp.float32),
            pltpu.VMEM((rows // LANES, LANES), jnp.float32),
            pltpu.VMEM(emb.shape, emb.dtype),
            pltpu.VMEM((cents, cols), cent.dtype),
        ],
        scratch_shapes=[
            pltpu.VMEM(cent.shape, cent.dtype),
            pltpu.VMEM((cents, LANES), jnp.float32),
            pltpu.SemaphoreType.DMA((3,)),
        ],
        compiler_params=params,
    )(in_hbm(emb), in_hbm(cent))

    other = lax.ppermute(lse, "core", [(0, 1), (1, 0)])
    top_lse = jnp.maximum(lse, other)
    chip = top_lse + jnp.log2(1.0 + jnp.exp2(jnp.minimum(lse, other) - top_lse))
    chips = math.prod(lax.axis_size(axis) for axis in EXCHANGE)
    every = lax.all_to_all(jnp.broadcast_to(chip, (chips,) + chip.shape), EXCHANGE, 0, 0)

    part = pltpu.VMEM((cents + MASS_ROWS, cols), jnp.bfloat16)
    first = n_dp // 2
    others = [k for k in range(1, n_dp) if k != first]
    far, w, mass, log_totals = pl.pallas_call(
        functools.partial(weights_kernel, first),
        in_specs=[IN_VMEM] * 4,
        out_specs=[IN_VMEM] * 4,
        out_shape=[
            part,
            pltpu.VMEM((cents, rows), jnp.bfloat16),
            pltpu.VMEM((MASS_ROWS, cols), jnp.bfloat16),
            jax.ShapeDtypeStruct(lse.shape, jnp.float32),
        ],
        compiler_params=params,
    )(in_vmem(p), in_vmem(top), in_vmem(every), in_vmem(emb_vmem))

    def send(p, shift):
        return lax.ppermute(p, "x", [(k, (k + shift) % n_dp) for k in range(n_dp)])

    near = pl.pallas_call(
        functools.partial(parts_kernel, others),
        in_specs=[IN_VMEM] * 3,
        out_specs=[IN_VMEM] * len(others),
        out_shape=[part] * len(others),
        compiler_params=params,
    )(in_vmem(w), in_vmem(emb_vmem), in_vmem(mass))
    own, own_mass = pl.pallas_call(
        own_kernel,
        in_specs=[IN_VMEM] * 5,
        out_specs=[IN_VMEM] * 2,
        out_shape=[pltpu.VMEM((cents, cols), jnp.float32), pltpu.VMEM((MASS_ROWS, cols), jnp.float32)],
        compiler_params=params,
    )(in_vmem(w), in_vmem(emb_vmem), in_vmem(prior), in_vmem(mass), in_vmem(send(far, first)))
    parts = [send(p, k) for k, p in zip(others, near)]
    new_centroids = pl.pallas_call(
        update_kernel,
        in_specs=[IN_VMEM] * (2 + len(parts)),
        out_specs=IN_VMEM,
        out_shape=jax.ShapeDtypeStruct((cents, cols), jnp.float32),
        compiler_params=params,
    )(in_vmem(own), in_vmem(own_mass), *[in_vmem(p) for p in parts])
    return new_centroids, log_totals.reshape(rows)


def solution(mesh):
    n_dp = mesh.shape["dp"]
    fine = Mesh(mesh.devices.reshape(n_dp, 4, 2, 4, 2), ("x", "z_hi", "z_lo", "y", "core"))
    cent = ("z_hi", "z_lo", "y", "core")
    return jax.shard_map(
        functools.partial(shards, n_dp),
        mesh=fine,
        in_specs=(P("x", None), P(cent, None)),
        out_specs=(P(cent, "x"), P("x")),
        check_vma=False,
    )
```

```python
import functools
import math

import jax
import jax.numpy as jnp
from jax import lax
from jax.experimental import pallas as pl
from jax.experimental.pallas import tpu as pltpu
from jax.sharding import Mesh, PartitionSpec as P

SOFTNESS = 0.1
PRIOR = 4.0
LOG2E = math.log2(math.e)
LN2 = math.log(2.0)
ROWS = 512
FIRST_LOAD = 512
LANES = 128
EXCHANGE = ("y", "z_lo", "z_hi")
MASS_ROWS = 16
VMEM_LIMIT = 16 * 1024 * 1024
IN_VMEM = pl.BlockSpec(memory_space=pltpu.VMEM)
IN_HBM = pl.BlockSpec(memory_space=pltpu.HBM)


def in_vmem(x):
    return pltpu.with_memory_space_constraint(x, pltpu.VMEM)


def in_hbm(x):
    return pltpu.with_memory_space_constraint(x, pltpu.HBM)


def logits_kernel(scale, emb_hbm, cent_hbm, p_ref, top_ref, lse_ref, emb_ref, prior_ref, cent_ref, half_sq, sems):
    rows = emb_ref.shape[0]
    cols = prior_ref.shape[1]
    cent_copy = pltpu.make_async_copy(cent_hbm, cent_ref, sems.at[0])
    cent_copy.start()
    copies = {}
    for start, end in ((0, FIRST_LOAD), (FIRST_LOAD, rows)):
        part = pl.ds(start, end - start)
        sem = sems.at[1 + len(copies)]
        copies[start] = pltpu.make_async_copy(emb_hbm.at[part, :], emb_ref.at[part, :], sem)
        copies[start].start()
    cent_copy.wait()
    c = cent_ref[...].astype(jnp.float32)
    half_sq[...] = jnp.broadcast_to(0.5 * jnp.sum(c * c, axis=1, keepdims=True), half_sq.shape)
    first_col = pl.multiple_of(lax.axis_index("x") * cols, cols)
    prior_ref[...] = cent_ref[:, pl.ds(first_col, cols)]
    for r in range(0, rows, ROWS):
        if r in copies:
            copies[r].wait()
        inner = lax.dot_general(
            cent_ref[...], emb_ref[r : r + ROWS, :], (((1,), (1,)), ((), ())), preferred_element_type=jnp.float32
        )
        z = (inner - half_sq[:, :1]) * scale
        top = jnp.max(z, axis=0, keepdims=True)
        p = jnp.exp2(z - top)
        p_ref[:, r : r + ROWS] = p
        lse = top + jnp.log2(jnp.sum(p, axis=0, keepdims=True))
        for k in range(ROWS // LANES):
            top_ref[pl.ds(r // LANES + k, 1), :] = top[:, k * LANES : (k + 1) * LANES]
            lse_ref[pl.ds(r // LANES + k, 1), :] = lse[:, k * LANES : (k + 1) * LANES]


def merge(lse):
    top = jnp.max(lse, axis=0)
    return top + jnp.log2(jnp.sum(jnp.exp2(lse - top), axis=0))


def weights_kernel(shift, p_ref, top_ref, every_ref, emb_ref, part_ref, w_ref, mass_ref, log_totals_ref):
    cents, rows = p_ref.shape
    cols = mass_ref.shape[1]
    totals = merge(every_ref[...])
    log_totals_ref[...] = totals * LN2
    factor = jnp.exp2(top_ref[...] - totals)
    masses = []
    for c in range(0, cents, 64):
        mass = jnp.zeros((64, LANES), jnp.float32)
        for k in range(rows // LANES):
            w = p_ref[c : c + 64, k * LANES : (k + 1) * LANES] * factor[k : k + 1, :]
            w_ref[c : c + 64, k * LANES : (k + 1) * LANES] = w.astype(jnp.bfloat16)
            mass = mass + w
        masses.append(mass)
    mass = jnp.concatenate(masses, axis=0)
    part_ref[:cents, :] = part_product(shift, w_ref, emb_ref).astype(jnp.bfloat16)
    mass = jnp.broadcast_to(jnp.sum(mass, axis=1, keepdims=True), (cents, LANES)).T
    half = MASS_ROWS // 2
    mass = jnp.concatenate([mass[:half, :cols], mass[:half, cols:]], axis=0).astype(jnp.bfloat16)
    mass_ref[...] = mass
    part_ref[cents:, :] = mass


def part_product(shift, w_ref, emb_ref):
    n_dp = lax.axis_size("x")
    cols = emb_ref.shape[1] // n_dp
    first_col = pl.multiple_of(lax.rem(lax.axis_index("x") + shift, n_dp) * cols, cols)
    return jnp.dot(w_ref[...], emb_ref[:, pl.ds(first_col, cols)], preferred_element_type=jnp.float32)


def parts_kernel(shifts, w_ref, emb_ref, mass_ref, *parts_refs):
    cents = w_ref.shape[0]
    for shift, part_ref in zip(shifts, parts_refs):
        part_ref[:cents, :] = part_product(shift, w_ref, emb_ref).astype(jnp.bfloat16)
        part_ref[cents:, :] = mass_ref[...]


def own_kernel(w_ref, emb_ref, prior_ref, mass_ref, far_ref, out_ref, out_mass_ref):
    cents = out_ref.shape[0]
    own = part_product(0, w_ref, emb_ref)
    out_ref[...] = own + PRIOR * prior_ref[...].astype(jnp.float32) + far_ref[:cents, :].astype(jnp.float32)
    out_mass_ref[...] = PRIOR + mass_ref[...].astype(jnp.float32) + far_ref[cents:, :].astype(jnp.float32)


def update_kernel(own_ref, mass_ref, *refs):
    parts_refs, out_ref = refs[:-1], refs[-1]
    cents, cols = out_ref.shape
    total = own_ref[...]
    mass = mass_ref[...]
    for part_ref in parts_refs:
        total = total + part_ref[:cents, :].astype(jnp.float32)
        mass = mass + part_ref[cents:, :].astype(jnp.float32)
    half = MASS_ROWS // 2
    inv = 1.0 / jnp.concatenate([mass[:1, :], mass[half : half + 1, :]], axis=1)
    inv = jnp.broadcast_to(inv, (LANES, cents)).T
    for k in range(cols // LANES):
        out_ref[:, k * LANES : (k + 1) * LANES] = total[:, k * LANES : (k + 1) * LANES] * inv


def shards(n_dp, emb, cent):
    rows, width = emb.shape
    cents = cent.shape[0]
    cols = width // n_dp
    scale = 2.0 * LOG2E / (SOFTNESS * math.sqrt(width))
    params = pltpu.CompilerParams(vmem_limit_bytes=VMEM_LIMIT)
    p, top, lse, emb_vmem, prior = pl.pallas_call(
        functools.partial(logits_kernel, scale),
        in_specs=[IN_HBM] * 2,
        out_specs=[IN_VMEM] * 5,
        out_shape=[
            pltpu.VMEM((cents, rows), jnp.float32),
            pltpu.VMEM((rows // LANES, LANES), jnp.float32),
            pltpu.VMEM((rows // LANES, LANES), jnp.float32),
            pltpu.VMEM(emb.shape, emb.dtype),
            pltpu.VMEM((cents, cols), cent.dtype),
        ],
        scratch_shapes=[
            pltpu.VMEM(cent.shape, cent.dtype),
            pltpu.VMEM((cents, LANES), jnp.float32),
            pltpu.SemaphoreType.DMA((3,)),
        ],
        compiler_params=params,
    )(in_hbm(emb), in_hbm(cent))

    other = lax.ppermute(lse, "core", [(0, 1), (1, 0)])
    top_lse = jnp.maximum(lse, other)
    chip = top_lse + jnp.log2(1.0 + jnp.exp2(jnp.minimum(lse, other) - top_lse))
    chips = math.prod(lax.axis_size(axis) for axis in EXCHANGE)
    every = lax.all_to_all(jnp.broadcast_to(chip, (chips,) + chip.shape), EXCHANGE, 0, 0)

    part = pltpu.VMEM((cents + MASS_ROWS, cols), jnp.bfloat16)
    first = n_dp // 2
    others = [k for k in range(1, n_dp) if k != first]
    far, w, mass, log_totals = pl.pallas_call(
        functools.partial(weights_kernel, first),
        in_specs=[IN_VMEM] * 4,
        out_specs=[IN_VMEM] * 4,
        out_shape=[
            part,
            pltpu.VMEM((cents, rows), jnp.bfloat16),
            pltpu.VMEM((MASS_ROWS, cols), jnp.bfloat16),
            jax.ShapeDtypeStruct(lse.shape, jnp.float32),
        ],
        compiler_params=params,
    )(in_vmem(p), in_vmem(top), in_vmem(every), in_vmem(emb_vmem))

    def send(p, shift):
        return lax.ppermute(p, "x", [(k, (k + shift) % n_dp) for k in range(n_dp)])

    near = pl.pallas_call(
        functools.partial(parts_kernel, others),
        in_specs=[IN_VMEM] * 3,
        out_specs=[IN_VMEM] * len(others),
        out_shape=[part] * len(others),
        compiler_params=params,
    )(in_vmem(w), in_vmem(emb_vmem), in_vmem(mass))
    own, own_mass = pl.pallas_call(
        own_kernel,
        in_specs=[IN_VMEM] * 5,
        out_specs=[IN_VMEM] * 2,
        out_shape=[pltpu.VMEM((cents, cols), jnp.float32), pltpu.VMEM((MASS_ROWS, cols), jnp.float32)],
        compiler_params=params,
    )(in_vmem(w), in_vmem(emb_vmem), in_vmem(prior), in_vmem(mass), in_vmem(send(far, first)))
    parts = [send(p, k) for k, p in zip(others, near)]
    new_centroids = pl.pallas_call(
        update_kernel,
        in_specs=[IN_VMEM] * (2 + len(parts)),
        out_specs=IN_VMEM,
        out_shape=jax.ShapeDtypeStruct((cents, cols), jnp.float32),
        compiler_params=params,
    )(in_vmem(own), in_vmem(own_mass), *[in_vmem(p) for p in parts])
    return new_centroids, log_totals.reshape(rows)


def solution(mesh):
    n_dp = mesh.shape["dp"]
    fine = Mesh(mesh.devices.reshape(n_dp, 4, 2, 4, 2), ("x", "z_hi", "z_lo", "y", "core"))
    cent = ("z_hi", "z_lo", "y", "core")
    return jax.shard_map(
        functools.partial(shards, n_dp),
        mesh=fine,
        in_specs=(P("x", None), P(cent, None)),
        out_specs=(P(cent, "x"), P("x")),
        check_vma=False,
    )
```
